32 devices in a mesh: groups: 2 (over y), side: 4 (over z), dev: 4 (over x, core).
Axes of the slice: x: 2, y: 2, z: 4, core: 2. Of those that a mesh axis runs over, the one named last changes fastest.
Arguments:
- tokens: bfloat16 [128, 7168], P(('groups', 'side', 'dev')), parts along dimension 0, may hold values from -6 to 6
- routes: int32 [128, 4], P(('groups', 'side', 'dev')), parts along dimension 0, may hold values from 0 to 7, all different within a row; in each aligned block of 4 rows (0 to 3, 4 to 7, ...) at most 3 rows name the same one
- gate_weights: bfloat16 [128, 4], P(('groups', 'side', 'dev')), parts along dimension 0, may hold values from 0.049804688 to 1
- experts_in: bfloat16 [8, 2, 7168, 2048], P('side', None, None, 'dev'), may hold values from -0.0625 to 0.0625
- experts_out: bfloat16 [8, 2048, 7168], P('side', 'dev'), may hold values from -0.125 to 0.125
- query_latent: bfloat16 [64, 128, 512], P(('groups', 'side', 'dev')), parts along dimension 0, may hold values from -8 to 8
- query_rope: bfloat16 [64, 64, 128], P(('groups', 'side', 'dev')), parts along dimension 0, may hold values from -8 to 8
- cache_latent: bfloat16 [64, 512, 512], P(('groups', 'side', 'dev')), parts along dimension 0, may hold values from -8 to 8
- cache_rope: bfloat16 [64, 64, 512], P(('groups', 'side', 'dev')), parts along dimension 0, may hold values from -8 to 8
- lengths: int32 [64], P(('groups', 'side', 'dev')), parts along dimension 0, may hold values from 64 to 512, as said below
Outputs:
- routed_out: bfloat16 [128, 7168], P(('groups', 'side', 'dev')), parts along dimension 0
- attended: bfloat16 [64, 128, 512], P(('groups', 'side', 'dev')), parts along dimension 0
The draws below stay inside these ranges and needn't reach their ends.
There are 2 independent parts, one for each index of `groups`. The reference program is written for one: setup_inputs(seed, part) draws one part's arguments, and reference() takes and returns one part's arrays. A program takes and returns all parts, laid end to end along the dimension named above; an argument that names none is the same for every part. Nothing has to cross between parts.
Inputs may be any that keep to these rules, and one draw needn't show every extreme that they name: `routes`: each row names 4 different experts. Among the 4 rows of one device no expert is named more than 3 times, and in every draw some device names some expert exactly 3 times. `lengths`: of every device's 2 requests one holds exactly 512 positions.
All inputs are finite; a program needn't handle non-finite values.
Results may differ from the reference program's by a relative error of at most 0.012.
Values may be sent and summed in bfloat16 or wider, within the bound.
No kernel may reach another device: no remote copies, remote signals or barrier semaphores. Data moves between devices by JAX's collectives and lax.ppermute only.
A program may use at most 128 MiB of HBM per device.

```python
import math
import jax
import jax.numpy as jnp
import numpy as np
from jax import lax

D = 7168
HID = 2048
HEADS = 128
LAT = 512
ROPE = 64
TOK_DEV = 4
ATT_REQ = 2
CTX = 512
EXP_NODE = 2
EXPERTS = 8
TOPK = 4
CAP = 3
TOKENS = 64
ATT = 32
N_SIDE = 4
N_DEV = 4


def draw_query_latent(key, part):
    key = jax.random.fold_in(key, 11)
    values_drawn = jnp.clip(1.5 * jax.random.normal(key, (ATT, HEADS, LAT)), -8.0, 8.0)
    return values_drawn.astype(jnp.bfloat16)


def draw_query_rope(key, part):
    key = jax.random.fold_in(key, 12)
    values_drawn = jnp.clip(1.5 * jax.random.normal(key, (ATT, ROPE, HEADS)), -8.0, 8.0)
    return values_drawn.astype(jnp.bfloat16)


def draw_cache_rope(key, part):
    key = jax.random.fold_in(key, 13)
    values_drawn = jnp.clip(jax.random.normal(key, (ATT, ROPE, CTX)), -8.0, 8.0)
    return values_drawn.astype(jnp.bfloat16)


def draw_lengths(key, part):
    key = jax.random.fold_in(key, 14)
    span_drawn = jax.random.randint(jax.random.fold_in(key, 1), (ATT,), CTX // 8, CTX + 1)
    longest = jax.random.randint(jax.random.fold_in(key, 2), (ATT // ATT_REQ,), 0, ATT_REQ)
    position = jnp.arange(ATT, dtype=jnp.int32) % ATT_REQ
    longest_slot = jnp.repeat(longest, ATT_REQ)
    return jnp.where(position == longest_slot, CTX, span_drawn).astype(jnp.int32)


def block_scale(own_key, shape, split, least, largest):
    def one(axis_at, parts):
        heights = jax.random.uniform(jax.random.fold_in(jax.random.fold_in(own_key, 6), axis_at), (parts,), jnp.float32, least / len(split), largest / len(split))
        return jnp.repeat(jnp.exp(heights), shape[axis_at] // parts).reshape((-1,) + (1,) * (len(shape) - axis_at - 1))

    factor_of = one(*split[0])
    for cut in split[1:]:
        factor_of = factor_of * one(*cut)
    return factor_of


def deal_out(stream_key, own, number, rows, number_of, top, limit, slope):
    sequence = jax.random.permutation(stream_key, number_of)
    crowded, common = portions_of(number_of, rows * top, limit, slope, True), portions_of(number_of, rows * top, limit, slope, False)
    places = jnp.arange(number_of)

    def named(tallies, rotation):
        used = int((tallies > 0).sum())
        fixed = max(1, used // 4)
        moved = fixed + (places - fixed + rotation * (used - fixed)) % max(1, number_of - fixed)
        return jnp.zeros((number_of,), jnp.int32).at[sequence[jnp.where(places < fixed, places, moved)]].set(jnp.asarray(tallies, jnp.int32))

    tallies = jnp.where(number % 4 == 0, named(crowded, number // 4), named(common, number - number // 4 - 1))
    mixed = jax.random.permutation(jax.random.fold_in(own, 3), number_of)
    giver, taker = mixed[0:number_of // 2 * 2:2], mixed[1:number_of // 2 * 2:2]
    margin = jnp.minimum(tallies[giver] - 1, limit - tallies[taker]) // 2
    margin = jnp.where((giver == sequence[0]) | (taker == sequence[0]) | (tallies[taker] == 0), 0, jnp.maximum(margin, 0))
    moved = jax.random.randint(jax.random.fold_in(own, 4), (number_of // 2,), 0, 1 << 20) % (margin + 1)
    tallies = tallies.at[giver].add(-moved).at[taker].add(moved)
    members = jnp.searchsorted(jnp.cumsum(tallies), jnp.arange(rows * top), side="right").astype(jnp.int32)
    grid = members.reshape(top, rows).T
    grid = grid[jax.random.permutation(jax.random.fold_in(own, 1), rows)]
    rotation = jax.random.randint(jax.random.fold_in(own, 2), (rows, 1), 0, top)
    return jnp.take_along_axis(grid, (jnp.arange(top)[None, :] + rotation) % top, axis=1)


def portions_of(number_of, total, reach, slope, full):
    portions = [(1 << 20) // math.isqrt(rank ** slope) + 1 for rank in range(1, number_of + 1)]
    largest = reach if full else min(reach, max(-(-total // number_of), total * portions[0] // sum(portions)))
    least = 1 if total - largest >= number_of - 1 else 0
    given, rest = [largest] + [least] * (number_of - 1), total - largest - least * (number_of - 1)
    while rest > 0:
        free = [i for i in range(1, number_of) if given[i] < largest] or [i for i in range(1, number_of) if given[i] < reach]
        pool, remaining = sum([portions[i] for i in free]), rest
        for i in free:
            addition = min(reach - given[i], max(1, remaining * portions[i] // pool), rest)
            given[i] = given[i] + addition
            rest = rest - addition
    return np.array(given)


def normal_values(stream_key, shape, scale, most, shards=(), kind=jnp.bfloat16):
    drawn = scale * jax.random.normal(stream_key, shape, jnp.float32)
    if shards:
        drawn = drawn * block_scale(stream_key, shape, shards, -0.22, 0.18)
    return jnp.clip(drawn, -most, most).astype(kind)


def setup_inputs(seed: int = 0, part: int = 0) -> dict:
    arg_keys = jax.random.split(jax.random.key(seed), 11)
    part_keys = jax.random.split(jax.random.fold_in(arg_keys[10], part), 11)
    tokens = normal_values(part_keys[0], (TOKENS, D), 1.0, 6.0, ((0, 16),))
    routes_keys = jax.random.split(jax.random.fold_in(part_keys[1], 1), TOKENS // TOK_DEV)
    routes_turns = jax.random.permutation(jax.random.fold_in(part_keys[1], 3), TOKENS // TOK_DEV)
    routes = jax.vmap(lambda own, number: deal_out(jax.random.fold_in(part_keys[1], 2), own, number, TOK_DEV, EXPERTS, TOPK, CAP, 2))(routes_keys, routes_turns).reshape((TOKENS, TOPK))
    gate_weights = jnp.clip(jnp.exp(math.log(1.0) - 2.9996462 * jax.random.uniform(part_keys[2], (TOKENS, TOPK), jnp.float32) ** block_scale(part_keys[2], (TOKENS, TOPK), ((0, 16),), -0.2, 0.2)), 0.049804688, 1.0).astype(jnp.bfloat16)
    experts_in = normal_values(arg_keys[3], (EXPERTS, 2, D, HID), D ** -0.5, 0.0625, ((0, 4), (3, 4)))
    experts_out = normal_values(arg_keys[4], (EXPERTS, HID, D), HID ** -0.5, 0.125, ((0, 4), (1, 4)))
    query_latent = draw_query_latent(jax.random.fold_in(jax.random.fold_in(arg_keys[10], part), 71), part)
    query_rope = draw_query_rope(jax.random.fold_in(jax.random.fold_in(arg_keys[10], part), 71), part)
    cache_latent = normal_values(part_keys[7], (ATT, CTX, LAT), 1.0, 8.0, ((0, 16),))
    cache_rope = draw_cache_rope(jax.random.fold_in(jax.random.fold_in(arg_keys[10], part), 71), part)
    lengths = draw_lengths(jax.random.fold_in(jax.random.fold_in(arg_keys[10], part), 71), part)
    return {"tokens": tokens, "routes": routes, "gate_weights": gate_weights, "experts_in": experts_in, "experts_out": experts_out, "query_latent": query_latent, "query_rope": query_rope, "cache_latent": cache_latent, "cache_rope": cache_rope, "lengths": lengths}


SCORE_SCALE = 192.0 ** -0.5


def reference(tokens, routes, gate_weights, experts_in, experts_out, query_latent, query_rope, cache_latent, cache_rope, lengths):
    block_width = HID // N_DEV
    gate_float = gate_weights.astype(jnp.float32)
    node_in = experts_in.reshape(N_SIDE, EXP_NODE, 2, D, HID)
    node_out = experts_out.reshape(N_SIDE, EXP_NODE, HID, D)
    node_ids = jnp.arange(EXPERTS, dtype=jnp.int32).reshape(N_SIDE, EXP_NODE)

    def one_node(running, packed):
        expert_ids, weights_in, weights_out = packed
        hidden_list = []
        weight_list = []
        for local in range(EXP_NODE):
            gate = jnp.dot(tokens, weights_in[local, 0], preferred_element_type=jnp.float32)
            upward = jnp.dot(tokens, weights_in[local, 1], preferred_element_type=jnp.float32)
            hidden_list.append((jax.nn.silu(gate) * upward).astype(jnp.bfloat16))
            weight_list.append(jnp.sum(jnp.where(routes == expert_ids[local], gate_float, jnp.zeros_like(gate_float)), axis=1))
        hidden = jnp.stack(hidden_list)
        weight = jnp.stack(weight_list)

        def one_block(total, block):
            start = (block * block_width).astype(jnp.int32)
            hidden_block = lax.dynamic_slice_in_dim(hidden, start, block_width, 2).astype(jnp.float32)
            out_block = lax.dynamic_slice_in_dim(weights_out, start, block_width, 1).astype(jnp.float32)
            product = jnp.einsum('eth,ehd->etd', hidden_block, out_block)
            term = jnp.sum(weight[:, :, None] * product, axis=0)
            term = lax.optimization_barrier(term.astype(jnp.bfloat16)).astype(jnp.float32)
            return total + term, None

        node_total, unused = lax.scan(one_block, jnp.zeros((TOKENS, D), jnp.float32), jnp.arange(N_DEV, dtype=jnp.int32))
        node_value = lax.optimization_barrier(node_total.astype(jnp.bfloat16)).astype(jnp.float32)
        return running + node_value, None

    routed_sum, unused = lax.scan(one_node, jnp.zeros((TOKENS, D), jnp.float32), (node_ids, node_in, node_out))
    routed_out = routed_sum.astype(jnp.bfloat16)

    def one_request(packed):
        query_one, rope_one, latent_one, keyrope_one, length = packed
        scores = jnp.dot(query_one, latent_one.T, preferred_element_type=jnp.float32)
        scores = (scores + jnp.dot(rope_one.T, keyrope_one, preferred_element_type=jnp.float32)) * SCORE_SCALE
        inside = jnp.arange(CTX, dtype=jnp.int32)[None, :] < length
        scores = jnp.where(inside, scores, -jnp.inf)
        highest = jnp.max(scores, axis=1, keepdims=True)
        shifted = jnp.exp(scores - highest)
        probability = (shifted / jnp.sum(shifted, axis=1, keepdims=True)).astype(jnp.bfloat16)
        return jnp.dot(probability, latent_one, preferred_element_type=jnp.float32).astype(jnp.bfloat16)

    attended = lax.map(one_request, (query_latent, query_rope, cache_latent, cache_rope, lengths))
    return routed_out, attended
```

```python
import functools

import jax
import jax.numpy as jnp
from jax import lax
from jax.experimental import pallas as pl
from jax.experimental.pallas import tpu as pltpu
from jax.sharding import PartitionSpec as P

SCORE_SCALE = 192.0 ** (-0.5)
BF16 = jnp.bfloat16
F32 = jnp.float32
LANES = 128


def swap(x, side_bits, dev_bits):
    side, dev = lax.axis_size("side"), lax.axis_size("dev")
    if side_bits == 0:
        return lax.ppermute(x, "dev", [(i, i ^ dev_bits) for i in range(dev)])
    if dev_bits == 0:
        return lax.ppermute(x, "side", [(i, i ^ side_bits) for i in range(side)])
    pairs = [(i, i ^ (side_bits * dev + dev_bits)) for i in range(side * dev)]
    return lax.ppermute(x, ("side", "dev"), pairs)


def pack_kernel(tokens, routes, gates, out):
    width = tokens.shape[1]
    out[:, :width] = tokens[...]
    pad = out.shape[1] - width
    lane = lax.broadcasted_iota(jnp.int32, (tokens.shape[0], pad), 1)
    total = jnp.zeros((tokens.shape[0], pad), F32)
    gate = gates[...].astype(F32)
    for k in range(routes.shape[1]):
        total = total + jnp.where(routes[:, k : k + 1] == lane, gate[:, k : k + 1], 0.0)
    out[:, width:] = total.astype(BF16)


def pack(tokens, routes, gates, experts):
    rows, width = tokens.shape
    pad = -(-experts // LANES) * LANES
    return pl.pallas_call(
        pack_kernel,
        out_shape=jax.ShapeDtypeStruct((rows, width + pad), BF16),
        compiler_params=pltpu.CompilerParams(vmem_limit_bytes=2 * 1024 * 1024),
        name="pack",
    )(tokens, routes, gates)


def chunks_of(width):
    step = 1024 if width % 1024 == 0 else width
    return step, width // step


def fetch_copies(e, w_in, held, sems):
    step, count = chunks_of(w_in.shape[2])
    return [
        pltpu.make_async_copy(
            w_in.at[e, g, pl.ds(i * step, step)], held.at[g, pl.ds(i * step, step)], sems.at[g * count + i]
        )
        for i in range(count)
        for g in range(2)
    ]


def fetch_kernel(e, w_in, held, sems):
    copies = fetch_copies(e, w_in, held, sems)
    for copy in copies:
        copy.start()
    for copy in copies:
        copy.wait()


def attend_kernel(
    e, lengths, w_in, queries, rope_queries, latents, ropes, held, attended, q, qr, c, cr, sems, own_sems
):
    own = [
        pltpu.make_async_copy(source, target, own_sems.at[i])
        for i, (source, target) in enumerate(((queries, q), (rope_queries, qr), (latents, c), (ropes, cr)))
    ]
    copies = fetch_copies(e, w_in, held, sems)
    for copy in own + copies:
        copy.start()
    for copy in own:
        copy.wait()
    for r in range(q.shape[0]):
        latent = c[r]
        scores = lax.dot_general(
            q[r], latent, (((1,), (1,)), ((), ())), preferred_element_type=F32
        ) + lax.dot_general(qr[r], cr[r], (((0,), (0,)), ((), ())), preferred_element_type=F32)
        scores = scores * SCORE_SCALE
        place = lax.broadcasted_iota(jnp.int32, scores.shape, 1)
        scores = jnp.where(place < lengths[r], scores, -jnp.inf)
        shifted = jnp.exp(scores - jnp.max(scores, axis=1, keepdims=True))
        shares = (shifted / jnp.sum(shifted, axis=1, keepdims=True)).astype(BF16)
        attended[r] = jnp.dot(shares, latent, preferred_element_type=F32).astype(BF16)
    for copy in copies:
        copy.wait()


def fetch(e, w_in, attention=None):
    _, _, width, block = w_in.shape
    sems = pltpu.SemaphoreType.DMA((2 * chunks_of(width)[1],))
    held = pltpu.VMEM((2, width, block), BF16)
    anywhere, vmem = pl.BlockSpec(memory_space=pltpu.HBM), pl.BlockSpec(memory_space=pltpu.VMEM)
    cost = pl.CostEstimate(flops=0, bytes_accessed=4 * width * block, transcendentals=0)
    if attention is None:
        return pl.pallas_call(
            functools.partial(fetch_kernel, e),
            out_shape=held,
            in_specs=[anywhere],
            out_specs=vmem,
            scratch_shapes=[sems],
            compiler_params=pltpu.CompilerParams(vmem_limit_bytes=2 * 1024 * 1024),
            cost_estimate=cost,
            name="fetch",
        )(in_hbm(w_in))
    arrays, lengths = attention[:-1], attention[-1]
    return pl.pallas_call(
        functools.partial(attend_kernel, e),
        out_shape=(held, jax.ShapeDtypeStruct(arrays[0].shape, BF16)),
        in_specs=[pl.BlockSpec(memory_space=pltpu.SMEM)] + [anywhere] * 5,
        out_specs=(vmem, vmem),
        scratch_shapes=[pltpu.VMEM(x.shape, BF16) for x in arrays] + [sems, pltpu.SemaphoreType.DMA((4,))],
        compiler_params=pltpu.CompilerParams(vmem_limit_bytes=8 * 1024 * 1024),
        cost_estimate=cost,
        name="attend",
    )(lengths, in_hbm(w_in), *[in_hbm(x) for x in arrays])


def experts_kernel(pieces, count, *refs):
    parts, refs = refs[:pieces], refs[pieces:]
    w_in, w_out, outs = refs[:count], refs[count], refs[count + 1 : -4]
    rows, act, held, sems = refs[-4:]
    _, block, width = w_out.shape
    step, chunks = chunks_of(width)
    copies = [
        pltpu.make_async_copy(w_out.at[:, :, pl.ds(i * step, step)], held.at[:, :, pl.ds(i * step, step)], sems.at[i])
        for i in range(chunks)
    ]
    for copy in copies:
        copy.start()
    size = parts[0].shape[0]
    for i, part in enumerate(parts):
        rows[i * size : (i + 1) * size, :] = part[...]
    first = lax.axis_index("side") * count
    gates = rows[:, width:].astype(F32)
    lane = lax.broadcasted_iota(jnp.int32, gates.shape, 1)
    for e in range(count):
        gate = jnp.dot(rows[:, :width], w_in[e][0], preferred_element_type=F32)
        up = jnp.dot(rows[:, :width], w_in[e][1], preferred_element_type=F32)
        weight = jnp.sum(jnp.where(lane == first + e, gates, 0.0), axis=1, keepdims=True)
        value = gate / (1.0 + jnp.exp(-gate)) * up * weight
        act[:, e * block : (e + 1) * block] = value.astype(BF16)
    for i, copy in enumerate(copies):
        copy.wait()
        at = slice(i * step, (i + 1) * step)
        total = jnp.dot(act[:, :block], held[0, :, at], preferred_element_type=F32)
        for e in range(1, count):
            total = total + jnp.dot(
                act[:, e * block : (e + 1) * block], held[e, :, at], preferred_element_type=F32
            )
        total = total.astype(BF16)
        start = 0
        for out in outs:
            out[:, at] = total[start : start + out.shape[0]]
            start += out.shape[0]


def in_hbm(x):
    return pltpu.with_memory_space_constraint(x, pltpu.HBM)


def in_vmem(x):
    return pltpu.with_memory_space_constraint(x, pltpu.VMEM)


def run_experts(near, far, w_in, w_out):
    parts = [*near, *far]
    size, packed = parts[0].shape
    total = size * len(parts)
    count, block, width = w_out.shape
    outs = [pltpu.VMEM((size, width), BF16) for _ in near] + [pltpu.VMEM((size * len(far), width), BF16)]
    whole = pl.BlockSpec(memory_space=pltpu.VMEM)
    results = pl.pallas_call(
        functools.partial(experts_kernel, len(parts), count),
        out_shape=outs,
        in_specs=[whole] * (len(parts) + count) + [pl.BlockSpec(memory_space=pltpu.HBM)],
        out_specs=[whole] * len(outs),
        scratch_shapes=[
            pltpu.VMEM((total, packed), BF16),
            pltpu.VMEM((total, count * block), BF16),
            pltpu.VMEM(w_out.shape, BF16),
            pltpu.SemaphoreType.DMA((chunks_of(width)[1],)),
        ],
        compiler_params=pltpu.CompilerParams(vmem_limit_bytes=24 * 1024 * 1024),
        cost_estimate=pl.CostEstimate(
            flops=6 * total * count * width * block, bytes_accessed=6 * count * width * block, transcendentals=0
        ),
        name="experts",
    )(*[in_vmem(x) for x in parts], *[in_vmem(w) for w in w_in], in_hbm(w_out))
    return results[:-1], results[-1]


def add(*terms):
    total = terms[0].astype(F32)
    for term in terms[1:]:
        total = total + term.astype(F32)
    return total.astype(BF16)


def shards(
    tokens,
    routes,
    gate_weights,
    experts_in,
    experts_out,
    query_latent,
    query_rope,
    cache_latent,
    cache_rope,
    lengths,
):
    side, dev = lax.axis_size("side"), lax.axis_size("dev")
    chips = dev // 2
    count = tokens.shape[0]
    packed = pack(tokens, routes, gate_weights, experts_in.shape[0] * side)
    attention = (query_latent, query_rope, cache_latent, cache_rope, lengths)
    first, attended = fetch(0, experts_in, attention)
    along = [packed] + [swap(packed, k, 0) for k in range(1, side)]
    *along, first, attended = lax.optimization_barrier((*along, first, attended))
    along = jnp.concatenate(along)
    near = [along] + [swap(along, 0, 2 * k) for k in range(1, chips)]
    others = [fetch(e, experts_in) for e in range(1, experts_in.shape[0])]
    far = [swap(near[0], 0, 1)]
    near, others = lax.optimization_barrier((near, others))
    far += [swap(piece, 0, 1) for piece in near[1:]]
    weights = [first] + others
    near_part, far_part = run_experts(near, far, weights, experts_out)
    far_part = swap(far_part, 0, 1)
    size = side * count
    both = [add(part, far_part[k * size : (k + 1) * size]) for k, part in enumerate(near_part)]
    column = add(both[0], *[swap(both[k], 0, 2 * k) for k in range(1, chips)])
    routed_out = add(
        column[:count],
        *[swap(column[k * count : (k + 1) * count], k, 0) for k in range(1, side)],
    )
    return (routed_out, attended)


def solution(mesh):
    return jax.shard_map(
        shards,
        mesh=mesh,
        in_specs=(
            P(("groups", "side", "dev"), None),
            P(("groups", "side", "dev"), None),
            P(("groups", "side", "dev"), None),
            P("side", None, None, "dev"),
            P("side", "dev", None),
            P(("groups", "side", "dev"), None, None),
            P(("groups", "side", "dev"), None, None),
            P(("groups", "side", "dev"), None, None),
            P(("groups", "side", "dev"), None, None),
            P(("groups", "side", "dev")),
        ),
        out_specs=(P(("groups", "side", "dev"), None), P(("groups", "side", "dev"), None, None)),
        check_vma=False,
    )
```

```python
import functools

import jax
import jax.numpy as jnp
from jax import lax
from jax.experimental import pallas as pl
from jax.experimental.pallas import tpu as pltpu
from jax.sharding import PartitionSpec as P

SCORE_SCALE = 192.0 ** (-0.5)
BF16 = jnp.bfloat16
F32 = jnp.float32
LANES = 128


def swap(x, side_bits, dev_bits):
    side, dev = lax.axis_size("side"), lax.axis_size("dev")
    if side_bits == 0:
        return lax.ppermute(x, "dev", [(i, i ^ dev_bits) for i in range(dev)])
    if dev_bits == 0:
        return lax.ppermute(x, "side", [(i, i ^ side_bits) for i in range(side)])
    pairs = [(i, i ^ (side_bits * dev + dev_bits)) for i in range(side * dev)]
    return lax.ppermute(x, ("side", "dev"), pairs)


def in_hbm(x):
    return pltpu.with_memory_space_constraint(x, pltpu.HBM)


def in_vmem(x):
    return pltpu.with_memory_space_constraint(x, pltpu.VMEM)


HBM = pl.BlockSpec(memory_space=pltpu.HBM)
VMEM = pl.BlockSpec(memory_space=pltpu.VMEM)
MIB = 1024 * 1024


def pack_kernel(tokens, routes, gates, out, tokens_here, routes_here, gates_here, sems):
    pairs = ((tokens, tokens_here), (routes, routes_here), (gates, gates_here))
    copies = [pltpu.make_async_copy(a, b, sems.at[i]) for i, (a, b) in enumerate(pairs)]
    for copy in copies:
        copy.start()
    for copy in copies:
        copy.wait()
    width = tokens.shape[1]
    out[:, :width] = tokens_here[...]
    lane = lax.broadcasted_iota(jnp.int32, (tokens.shape[0], out.shape[1] - width), 1)
    total = jnp.zeros(lane.shape, F32)
    gate = gates_here[...].astype(F32)
    for k in range(routes.shape[1]):
        total = total + jnp.where(routes_here[:, k : k + 1] == lane, gate[:, k : k + 1], 0.0)
    out[:, width:] = total.astype(BF16)


def pack(tokens, routes, gates, experts):
    rows, width = tokens.shape
    pad = -(-experts // LANES) * LANES
    arrays = (tokens, routes, gates)
    return pl.pallas_call(
        pack_kernel,
        out_shape=pltpu.VMEM((rows, width + pad), BF16),
        in_specs=[HBM] * 3,
        out_specs=VMEM,
        scratch_shapes=[pltpu.VMEM(x.shape, x.dtype) for x in arrays] + [pltpu.SemaphoreType.DMA((3,))],
        compiler_params=pltpu.CompilerParams(vmem_limit_bytes=2 * MIB),
        name="pack",
    )(*[in_hbm(x) for x in arrays])


def chunks_of(width):
    step = 1024 if width % 1024 == 0 else width
    return step, width // step


def fetch_copies(e, w_in, held, sems):
    step, count = chunks_of(w_in.shape[2])
    return [
        pltpu.make_async_copy(
            w_in.at[e, g, pl.ds(i * step, step)], held.at[g, pl.ds(i * step, step)], sems.at[g * count + i]
        )
        for i in range(count)
        for g in range(2)
    ]


def fetch_kernel(e, w_in, held, sems):
    copies = fetch_copies(e, w_in, held, sems)
    for copy in copies:
        copy.start()
    for copy in copies:
        copy.wait()


def fetch(e, w_in):
    _, _, width, block = w_in.shape
    return pl.pallas_call(
        functools.partial(fetch_kernel, e),
        out_shape=pltpu.VMEM((2, width, block), BF16),
        in_specs=[HBM],
        out_specs=VMEM,
        scratch_shapes=[pltpu.SemaphoreType.DMA((2 * chunks_of(width)[1],))],
        compiler_params=pltpu.CompilerParams(vmem_limit_bytes=2 * MIB),
        cost_estimate=pl.CostEstimate(flops=0, bytes_accessed=FETCH_COST * 4 * width * block, transcendentals=0),
        name="fetch",
    )(in_hbm(w_in))


FETCH_COST = 0


def attend_kernel(lengths, queries, rope_queries, latents, ropes, attended, q, qr, c, cr, out, sems, out_sems):
    pairs = ((queries, q), (rope_queries, qr), (latents, c), (ropes, cr))
    count = q.shape[0]
    copies = [
        [pltpu.make_async_copy(a.at[r], b.at[r], sems.at[r, i]) for i, (a, b) in enumerate(pairs)]
        for r in range(count)
    ]
    for request in copies:
        for copy in request:
            copy.start()
    results = []
    for r in range(count):
        for copy in copies[r]:
            copy.wait()
        latent = c[r]
        scores = lax.dot_general(
            q[r], latent, (((1,), (1,)), ((), ())), preferred_element_type=F32
        ) + lax.dot_general(qr[r], cr[r], (((0,), (0,)), ((), ())), preferred_element_type=F32)
        scores = scores * SCORE_SCALE
        place = lax.broadcasted_iota(jnp.int32, scores.shape, 1)
        scores = jnp.where(place < lengths[r], scores, -jnp.inf)
        shifted = jnp.exp(scores - jnp.max(scores, axis=1, keepdims=True))
        shares = (shifted / jnp.sum(shifted, axis=1, keepdims=True)).astype(BF16)
        out[r] = jnp.dot(shares, latent, preferred_element_type=F32).astype(BF16)
        results.append(pltpu.make_async_copy(out.at[r], attended.at[r], out_sems.at[r]))
        results[-1].start()
    for copy in results:
        copy.wait()


def attend(query_latent, query_rope, cache_latent, cache_rope, lengths):
    arrays = (query_latent, query_rope, cache_latent, cache_rope)
    count = query_latent.shape[0]
    return pl.pallas_call(
        attend_kernel,
        out_shape=pltpu.HBM(query_latent.shape, BF16),
        in_specs=[pl.BlockSpec(memory_space=pltpu.SMEM)] + [HBM] * 4,
        out_specs=HBM,
        scratch_shapes=[pltpu.VMEM(x.shape, BF16) for x in (*arrays, query_latent)]
        + [pltpu.SemaphoreType.DMA((count, 4)), pltpu.SemaphoreType.DMA((count,))],
        compiler_params=pltpu.CompilerParams(vmem_limit_bytes=8 * MIB),
        name="attend",
    )(in_hbm(lengths), *[in_hbm(x) for x in arrays])


def experts_kernel(pieces, count, *refs):
    parts, refs = refs[:pieces], refs[pieces:]
    w_in, held, outs = refs[:count], refs[count], refs[count + 1 : -2]
    rows, act = refs[-2:]
    _, block, width = held.shape
    step, chunks = chunks_of(width)
    size = parts[0].shape[0]
    for i, part in enumerate(parts):
        rows[i * size : (i + 1) * size, :] = part[...]
    first = lax.axis_index("side") * count
    gates = rows[:, width:].astype(F32)
    lane = lax.broadcasted_iota(jnp.int32, gates.shape, 1)
    for e in range(count):
        gate = jnp.dot(rows[:, :width], w_in[e][0], preferred_element_type=F32)
        up = jnp.dot(rows[:, :width], w_in[e][1], preferred_element_type=F32)
        weight = jnp.sum(jnp.where(lane == first + e, gates, 0.0), axis=1, keepdims=True)
        value = gate / (1.0 + jnp.exp(-gate)) * up * weight
        act[:, e * block : (e + 1) * block] = value.astype(BF16)
    for i in range(chunks):
        at = slice(i * step, (i + 1) * step)
        total = jnp.dot(act[:, :block], held[0, :, at], preferred_element_type=F32)
        for e in range(1, count):
            total = total + jnp.dot(
                act[:, e * block : (e + 1) * block], held[e, :, at], preferred_element_type=F32
            )
        total = total.astype(BF16)
        start = 0
        for out in outs:
            out[:, at] = total[start : start + out.shape[0]]
            start += out.shape[0]


def run_experts(near, far, w_in, w_out):
    parts = [*near, *far]
    size, packed = parts[0].shape
    total = size * len(parts)
    count, block, width = w_out.shape
    room = 2 * MIB + total * (2 * packed + 2 * count * block + 8 * chunks_of(width)[0])
    outs = [pltpu.VMEM((size, width), BF16) for _ in near] + [pltpu.VMEM((size * len(far), width), BF16)]
    results = pl.pallas_call(
        functools.partial(experts_kernel, len(parts), count),
        out_shape=outs,
        in_specs=[VMEM] * (len(parts) + count + 1),
        out_specs=[VMEM] * len(outs),
        scratch_shapes=[
            pltpu.VMEM((total, packed), BF16),
            pltpu.VMEM((total, count * block), BF16),
        ],
        compiler_params=pltpu.CompilerParams(vmem_limit_bytes=room),
        cost_estimate=pl.CostEstimate(
            flops=6 * total * count * width * block, bytes_accessed=6 * count * width * block, transcendentals=0
        ),
        name="experts",
    )(*[in_vmem(x) for x in parts], *[in_vmem(w) for w in w_in], w_out)
    return results[:-1], results[-1]


def add(*terms):
    total = terms[0].astype(F32)
    for term in terms[1:]:
        total = total + term.astype(F32)
    return total.astype(BF16)


def shards(
    tokens,
    routes,
    gate_weights,
    experts_in,
    experts_out,
    query_latent,
    query_rope,
    cache_latent,
    cache_rope,
    lengths,
):
    side, dev = lax.axis_size("side"), lax.axis_size("dev")
    chips = dev // 2
    count = tokens.shape[0]
    packed = pack(tokens, routes, gate_weights, experts_in.shape[0] * side)
    along = [packed] + [swap(packed, k, 0) for k in range(1, side)]
    first = fetch(0, experts_in)
    *along, first = lax.optimization_barrier((*along, first))
    along = jnp.concatenate(along)
    near = [along] + [swap(along, 0, 2 * k) for k in range(1, chips)]
    others = [fetch(e, experts_in) for e in range(1, experts_in.shape[0])]
    far = [swap(near[0], 0, 1)]
    near, others = lax.optimization_barrier((near, others))
    far += [swap(piece, 0, 1) for piece in near[1:]]
    weights = [first] + others
    near_part, far_part = run_experts(near, far, weights, experts_out)
    far_part = swap(far_part, 0, 1)
    size = side * count
    both = [add(part, far_part[k * size : (k + 1) * size]) for k, part in enumerate(near_part)]
    across = [swap(both[k], 0, 2 * k) for k in range(1, chips)]
    attended = attend(query_latent, query_rope, cache_latent, cache_rope, lengths)
    across, attended = lax.optimization_barrier((across, attended))
    column = add(both[0], *across)
    routed_out = add(
        column[:count],
        *[swap(column[k * count : (k + 1) * count], k, 0) for k in range(1, side)],
    )
    return (routed_out, attended)


def solution(mesh):
    return jax.shard_map(
        shards,
        mesh=mesh,
        in_specs=(
            P(("groups", "side", "dev"), None),
            P(("groups", "side", "dev"), None),
            P(("groups", "side", "dev"), None),
            P("side", None, None, "dev"),
            P("side", "dev", None),
            P(("groups", "side", "dev"), None, None),
            P(("groups", "side", "dev"), None, None),
            P(("groups", "side", "dev"), None, None),
            P(("groups", "side", "dev"), None, None),
            P(("groups", "side", "dev")),
        ),
        out_specs=(P(("groups", "side", "dev"), None), P(("groups", "side", "dev"), None, None)),
        check_vma=False,
    )
```

```python
import functools

import jax
import jax.numpy as jnp
from jax import lax
from jax.experimental import pallas as pl
from jax.experimental.pallas import tpu as pltpu
from jax.sharding import PartitionSpec as P

SCORE_SCALE = 192.0 ** (-0.5)
BF16 = jnp.bfloat16
F32 = jnp.float32
LANES = 128


def swap(x, side_bits, dev_bits):
    side, dev = lax.axis_size("side"), lax.axis_size("dev")
    if side_bits == 0:
        return lax.ppermute(x, "dev", [(i, i ^ dev_bits) for i in range(dev)])
    if dev_bits == 0:
        return lax.ppermute(x, "side", [(i, i ^ side_bits) for i in range(side)])
    pairs = [(i, i ^ (side_bits * dev + dev_bits)) for i in range(side * dev)]
    return lax.ppermute(x, ("side", "dev"), pairs)


def in_hbm(x):
    return pltpu.with_memory_space_constraint(x, pltpu.HBM)


def in_vmem(x):
    return pltpu.with_memory_space_constraint(x, pltpu.VMEM)


HBM = pl.BlockSpec(memory_space=pltpu.HBM)
VMEM = pl.BlockSpec(memory_space=pltpu.VMEM)
MIB = 1024 * 1024


def pack_kernel(tokens, routes, gates, out, tokens_here, routes_here, gates_here, sems):
    pairs = ((tokens, tokens_here), (routes, routes_here), (gates, gates_here))
    copies = [pltpu.make_async_copy(a, b, sems.at[i]) for i, (a, b) in enumerate(pairs)]
    for copy in copies:
        copy.start()
    for copy in copies:
        copy.wait()
    width = tokens.shape[1]
    out[:, :width] = tokens_here[...]
    lane = lax.broadcasted_iota(jnp.int32, (tokens.shape[0], out.shape[1] - width), 1)
    total = jnp.zeros(lane.shape, F32)
    gate = gates_here[...].astype(F32)
    for k in range(routes.shape[1]):
        total = total + jnp.where(routes_here[:, k : k + 1] == lane, gate[:, k : k + 1], 0.0)
    out[:, width:] = total.astype(BF16)


def pack(tokens, routes, gates, experts):
    rows, width = tokens.shape
    pad = -(-experts // LANES) * LANES
    arrays = (tokens, routes, gates)
    return pl.pallas_call(
        pack_kernel,
        out_shape=pltpu.VMEM((rows, width + pad), BF16),
        in_specs=[HBM] * 3,
        out_specs=VMEM,
        scratch_shapes=[pltpu.VMEM(x.shape, x.dtype) for x in arrays] + [pltpu.SemaphoreType.DMA((3,))],
        compiler_params=pltpu.CompilerParams(vmem_limit_bytes=2 * MIB),
        name="pack",
    )(*[in_hbm(x) for x in arrays])


def chunks_of(width):
    step = 1024 if width % 1024 == 0 else width
    return step, width // step


def fetch_kernel(e, first, w_in, *refs):
    held, sems = refs[-2:]
    step, _ = chunks_of(w_in.shape[2])
    copies = [
        pltpu.make_async_copy(
            w_in.at[e, g, pl.ds((first + i) * step, step)], held.at[g, pl.ds(i * step, step)], sems.at[g, i]
        )
        for i in range(held.shape[1] // step)
        for g in range(2)
    ]
    for copy in copies:
        copy.start()
    for copy in copies:
        copy.wait()


def fetch(w_in, e, first, count, *ready):
    _, _, width, block = w_in.shape
    step, _ = chunks_of(width)
    return pl.pallas_call(
        functools.partial(fetch_kernel, e, first),
        out_shape=pltpu.VMEM((2, count * step, block), BF16),
        in_specs=[HBM] + [VMEM] * len(ready),
        out_specs=VMEM,
        scratch_shapes=[pltpu.SemaphoreType.DMA((2, count))],
        compiler_params=pltpu.CompilerParams(vmem_limit_bytes=2 * MIB),
        name="fetch",
    )(in_hbm(w_in), *ready)


def attend_kernel(lengths, queries, rope_queries, latents, ropes, attended, q, qr, c, cr, out, sems, out_sems):
    pairs = ((queries, q), (rope_queries, qr), (latents, c), (ropes, cr))
    count = q.shape[0]
    copies = [
        [pltpu.make_async_copy(a.at[r], b.at[r], sems.at[r, i]) for i, (a, b) in enumerate(pairs)]
        for r in range(count)
    ]
    for request in copies:
        for copy in request:
            copy.start()
    results = []
    for r in range(count):
        for copy in copies[r]:
            copy.wait()
        latent = c[r]
        scores = lax.dot_general(
            q[r], latent, (((1,), (1,)), ((), ())), preferred_element_type=F32
        ) + lax.dot_general(qr[r], cr[r], (((0,), (0,)), ((), ())), preferred_element_type=F32)
        scores = scores * SCORE_SCALE
        place = lax.broadcasted_iota(jnp.int32, scores.shape, 1)
        scores = jnp.where(place < lengths[r], scores, -jnp.inf)
        shifted = jnp.exp(scores - jnp.max(scores, axis=1, keepdims=True))
        shares = (shifted / jnp.sum(shifted, axis=1, keepdims=True)).astype(BF16)
        out[r] = jnp.dot(shares, latent, preferred_element_type=F32).astype(BF16)
        results.append(pltpu.make_async_copy(out.at[r], attended.at[r], out_sems.at[r]))
        results[-1].start()
    for copy in results:
        copy.wait()


def attend(query_latent, query_rope, cache_latent, cache_rope, lengths):
    arrays = (query_latent, query_rope, cache_latent, cache_rope)
    count = query_latent.shape[0]
    return pl.pallas_call(
        attend_kernel,
        out_shape=pltpu.HBM(query_latent.shape, BF16),
        in_specs=[pl.BlockSpec(memory_space=pltpu.SMEM)] + [HBM] * 4,
        out_specs=HBM,
        scratch_shapes=[pltpu.VMEM(x.shape, BF16) for x in (*arrays, query_latent)]
        + [pltpu.SemaphoreType.DMA((count, 4)), pltpu.SemaphoreType.DMA((count,))],
        compiler_params=pltpu.CompilerParams(vmem_limit_bytes=8 * MIB),
        name="attend",
    )(in_hbm(lengths), *[in_hbm(x) for x in arrays])


def project(rows, parts, g):
    total, start = None, 0
    for part in parts:
        size = part.shape[1]
        term = jnp.dot(rows[:, start : start + size], part[g], preferred_element_type=F32)
        total = term if total is None else total + term
        start += size
    return total


def experts_kernel(pieces, held_parts, *refs):
    parts, refs = refs[:pieces], refs[pieces:]
    count = sum(held_parts)
    flat, held, outs = refs[:count], refs[count], refs[count + 1 : -2]
    rows, act = refs[-2:]
    w_in, start = [], 0
    for number in held_parts:
        w_in.append(flat[start : start + number])
        start += number
    count, block, width = held.shape
    step, chunks = chunks_of(width)
    size = parts[0].shape[0]
    for i, part in enumerate(parts):
        rows[i * size : (i + 1) * size, :] = part[...]
    first = lax.axis_index("side") * count
    gates = rows[:, width:].astype(F32)
    lane = lax.broadcasted_iota(jnp.int32, gates.shape, 1)
    for e in range(count):
        gate, up = [project(rows, w_in[e], g) for g in range(2)]
        weight = jnp.sum(jnp.where(lane == first + e, gates, 0.0), axis=1, keepdims=True)
        value = gate / (1.0 + jnp.exp(-gate)) * up * weight
        act[:, e * block : (e + 1) * block] = value.astype(BF16)
    for i in range(chunks):
        at = slice(i * step, (i + 1) * step)
        total = jnp.dot(act[:, :block], held[0, :, at], preferred_element_type=F32)
        for e in range(1, count):
            total = total + jnp.dot(
                act[:, e * block : (e + 1) * block], held[e, :, at], preferred_element_type=F32
            )
        total = total.astype(BF16)
        start = 0
        for out in outs:
            out[:, at] = total[start : start + out.shape[0]]
            start += out.shape[0]


def run_experts(near, far, w_in, w_out):
    parts = [*near, *far]
    size, packed = parts[0].shape
    total = size * len(parts)
    count, block, width = w_out.shape
    room = 2 * MIB + total * (2 * packed + 2 * count * block + 8 * chunks_of(width)[0])
    outs = [pltpu.VMEM((size, width), BF16) for _ in parts]
    results = pl.pallas_call(
        functools.partial(experts_kernel, len(parts), tuple(len(x) for x in w_in)),
        out_shape=outs,
        in_specs=[VMEM] * (len(parts) + sum(len(x) for x in w_in) + 1),
        out_specs=[VMEM] * len(outs),
        scratch_shapes=[
            pltpu.VMEM((total, packed), BF16),
            pltpu.VMEM((total, count * block), BF16),
        ],
        compiler_params=pltpu.CompilerParams(vmem_limit_bytes=room),
        cost_estimate=pl.CostEstimate(
            flops=6 * total * count * width * block, bytes_accessed=6 * count * width * block, transcendentals=0
        ),
        name="experts",
    )(*[in_vmem(x) for x in parts], *[in_vmem(w) for x in w_in for w in x], w_out)
    return results[: len(near)], results[len(near) :]


def add(*terms):
    total = terms[0].astype(F32)
    for term in terms[1:]:
        total = total + term.astype(F32)
    return total.astype(BF16)


def shards(
    tokens,
    routes,
    gate_weights,
    experts_in,
    experts_out,
    query_latent,
    query_rope,
    cache_latent,
    cache_rope,
    lengths,
):
    side, dev = lax.axis_size("side"), lax.axis_size("dev")
    chips = dev // 2
    count = tokens.shape[0]
    packed = pack(tokens, routes, gate_weights, experts_in.shape[0] * side)
    chunks = chunks_of(tokens.shape[1])[1]
    last = 1 if chunks > 2 else 0
    along = [packed] + [swap(packed, k, 0) for k in range(1, side)]
    first = fetch(experts_in, 0, 0, chunks - last)
    *along, first = lax.optimization_barrier((*along, first))
    along = jnp.concatenate(along)
    near = [along] + [swap(along, 0, 2 * k) for k in range(1, chips)]
    others = [fetch(experts_in, e, 0, chunks, experts_out) for e in range(1, experts_in.shape[0])]
    far = [swap(near[0], 0, 1)]
    near, others = lax.optimization_barrier((near, others))
    far += [swap(piece, 0, 1) for piece in near[1:]]
    weights = [[first]] + [[x] for x in others]
    if last:
        near, rest = lax.optimization_barrier((near, experts_in))
        weights[0].append(fetch(rest, 0, chunks - last, last))
    near_part, far_part = run_experts(near, far, weights, experts_out)
    both = [add(near_part[k], swap(far_part[k], 0, 1)) for k in range(1, chips)]
    own_far, both = lax.optimization_barrier((far_part[0], both))
    across = [swap(both[k - 1], 0, 2 * k) for k in range(1, chips)]
    own = add(near_part[0], swap(own_far, 0, 1))
    attended = attend(query_latent, query_rope, cache_latent, cache_rope, lengths)
    across, attended = lax.optimization_barrier((across, attended))
    column = add(own, *across)
    routed_out = add(
        column[:count],
        *[swap(column[k * count : (k + 1) * count], k, 0) for k in range(1, side)],
    )
    return (routed_out, attended)


def solution(mesh):
    return jax.shard_map(
        shards,
        mesh=mesh,
        in_specs=(
            P(("groups", "side", "dev"), None),
            P(("groups", "side", "dev"), None),
            P(("groups", "side", "dev"), None),
            P("side", None, None, "dev"),
            P("side", "dev", None),
            P(("groups", "side", "dev"), None, None),
            P(("groups", "side", "dev"), None, None),
            P(("groups", "side", "dev"), None, None),
            P(("groups", "side", "dev"), None, None),
            P(("groups", "side", "dev")),
        ),
        out_specs=(P(("groups", "side", "dev"), None), P(("groups", "side", "dev"), None, None)),
        check_vma=False,
    )
```

```python
import functools

import jax
import jax.numpy as jnp
from jax import lax
from jax.experimental import pallas as pl
from jax.experimental.pallas import tpu as pltpu
from jax.sharding import PartitionSpec as P

SCORE_SCALE = 192.0 ** (-0.5)
BF16 = jnp.bfloat16
F32 = jnp.float32
LANES = 128


def swap(x, side_bits, dev_bits):
    side, dev = lax.axis_size("side"), lax.axis_size("dev")
    if side_bits == 0:
        return lax.ppermute(x, "dev", [(i, i ^ dev_bits) for i in range(dev)])
    if dev_bits == 0:
        return lax.ppermute(x, "side", [(i, i ^ side_bits) for i in range(side)])
    pairs = [(i, i ^ (side_bits * dev + dev_bits)) for i in range(side * dev)]
    return lax.ppermute(x, ("side", "dev"), pairs)


def in_hbm(x):
    return pltpu.with_memory_space_constraint(x, pltpu.HBM)


def in_vmem(x):
    return pltpu.with_memory_space_constraint(x, pltpu.VMEM)


HBM = pl.BlockSpec(memory_space=pltpu.HBM)
VMEM = pl.BlockSpec(memory_space=pltpu.VMEM)
MIB = 1024 * 1024


def pack_kernel(tokens, routes, gates, out, routes_here, gates_here, sems):
    width = tokens.shape[1]
    pairs = ((tokens, out.at[:, :width]), (routes, routes_here), (gates, gates_here))
    copies = [pltpu.make_async_copy(a, b, sems.at[i]) for i, (a, b) in enumerate(pairs)]
    for copy in copies:
        copy.start()
    for copy in copies[1:]:
        copy.wait()
    lane = lax.broadcasted_iota(jnp.int32, (tokens.shape[0], out.shape[1] - width), 1)
    total = jnp.zeros(lane.shape, F32)
    gate = gates_here[...].astype(F32)
    for k in range(routes.shape[1]):
        total = total + jnp.where(routes_here[:, k : k + 1] == lane, gate[:, k : k + 1], 0.0)
    out[:, width:] = total.astype(BF16)
    copies[0].wait()


def pack(tokens, routes, gates, experts):
    rows, width = tokens.shape
    pad = -(-experts // LANES) * LANES
    arrays = (tokens, routes, gates)
    return pl.pallas_call(
        pack_kernel,
        out_shape=pltpu.VMEM((rows, width + pad), BF16),
        in_specs=[HBM] * 3,
        out_specs=VMEM,
        scratch_shapes=[pltpu.VMEM(x.shape, x.dtype) for x in arrays[1:]] + [pltpu.SemaphoreType.DMA((3,))],
        compiler_params=pltpu.CompilerParams(vmem_limit_bytes=2 * MIB),
        name="pack",
    )(*[in_hbm(x) for x in arrays])


def chunks_of(width):
    step = 1024 if width % 1024 == 0 else width
    return step, width // step


def fetch_kernel(e, first, w_in, *refs):
    held, sems = refs[-2:]
    step, _ = chunks_of(w_in.shape[2])
    copies = [
        pltpu.make_async_copy(
            w_in.at[e, g, pl.ds((first + i) * step, step)], held.at[g, pl.ds(i * step, step)], sems.at[g, i]
        )
        for i in range(held.shape[1] // step)
        for g in range(2)
    ]
    for copy in copies:
        copy.start()
    for copy in copies:
        copy.wait()


def fetch(w_in, e, first, count, *ready):
    _, _, width, block = w_in.shape
    step, _ = chunks_of(width)
    return pl.pallas_call(
        functools.partial(fetch_kernel, e, first),
        out_shape=pltpu.VMEM((2, count * step, block), BF16),
        in_specs=[HBM] + [VMEM] * len(ready),
        out_specs=VMEM,
        scratch_shapes=[pltpu.SemaphoreType.DMA((2, count))],
        compiler_params=pltpu.CompilerParams(vmem_limit_bytes=2 * MIB),
        name="fetch",
    )(in_hbm(w_in), *ready)


def attend_kernel(lengths, queries, rope_queries, latents, ropes, attended, q, qr, c, cr, out, sems, out_sems):
    pairs = ((queries, q), (rope_queries, qr), (latents, c), (ropes, cr))
    count = q.shape[0]
    copies = [
        [pltpu.make_async_copy(a.at[r], b.at[r], sems.at[r, i]) for i, (a, b) in enumerate(pairs)]
        for r in range(count)
    ]
    for request in copies:
        for copy in request:
            copy.start()
    results = []
    for r in range(count):
        for copy in copies[r]:
            copy.wait()
        latent = c[r]
        scores = lax.dot_general(
            q[r], latent, (((1,), (1,)), ((), ())), preferred_element_type=F32
        ) + lax.dot_general(qr[r], cr[r], (((0,), (0,)), ((), ())), preferred_element_type=F32)
        scores = scores * SCORE_SCALE
        place = lax.broadcasted_iota(jnp.int32, scores.shape, 1)
        scores = jnp.where(place < lengths[r], scores, -jnp.inf)
        shifted = jnp.exp(scores - jnp.max(scores, axis=1, keepdims=True))
        shares = (shifted / jnp.sum(shifted, axis=1, keepdims=True)).astype(BF16)
        out[r] = jnp.dot(shares, latent, preferred_element_type=F32).astype(BF16)
        results.append(pltpu.make_async_copy(out.at[r], attended.at[r], out_sems.at[r]))
        results[-1].start()
    for copy in results:
        copy.wait()


def attend(query_latent, query_rope, cache_latent, cache_rope, lengths):
    arrays = (query_latent, query_rope, cache_latent, cache_rope)
    count = query_latent.shape[0]
    return pl.pallas_call(
        attend_kernel,
        out_shape=pltpu.HBM(query_latent.shape, BF16),
        in_specs=[pl.BlockSpec(memory_space=pltpu.SMEM)] + [HBM] * 4,
        out_specs=HBM,
        scratch_shapes=[pltpu.VMEM(x.shape, BF16) for x in (*arrays, query_latent)]
        + [pltpu.SemaphoreType.DMA((count, 4)), pltpu.SemaphoreType.DMA((count,))],
        compiler_params=pltpu.CompilerParams(vmem_limit_bytes=8 * MIB),
        name="attend",
    )(in_hbm(lengths), *[in_hbm(x) for x in arrays])


def project(rows, parts, g):
    total, start = None, 0
    for part in parts:
        size = part.shape[1]
        term = jnp.dot(rows[:, start : start + size], part[g], preferred_element_type=F32)
        total = term if total is None else total + term
        start += size
    return total


def experts_kernel(pieces, held_parts, *refs):
    parts, refs = refs[:pieces], refs[pieces:]
    count = sum(held_parts)
    flat, held, outs = refs[:count], refs[count], refs[count + 1 : -2]
    rows, act = refs[-2:]
    w_in, start = [], 0
    for number in held_parts:
        w_in.append(flat[start : start + number])
        start += number
    count, block, width = held.shape
    step, chunks = chunks_of(width)
    size = parts[0].shape[0]
    for i, part in enumerate(parts):
        rows[i * size : (i + 1) * size, :] = part[...]
    first = lax.axis_index("side") * count
    gates = rows[:, width:].astype(F32)
    lane = lax.broadcasted_iota(jnp.int32, gates.shape, 1)
    for e in range(count):
        gate, up = [project(rows, w_in[e], g) for g in range(2)]
        weight = jnp.sum(jnp.where(lane == first + e, gates, 0.0), axis=1, keepdims=True)
        value = gate / (1.0 + jnp.exp(-gate)) * up * weight
        act[:, e * block : (e + 1) * block] = value.astype(BF16)
    for i in range(chunks):
        at = slice(i * step, (i + 1) * step)
        total = jnp.dot(act[:, :block], held[0, :, at], preferred_element_type=F32)
        for e in range(1, count):
            total = total + jnp.dot(
                act[:, e * block : (e + 1) * block], held[e, :, at], preferred_element_type=F32
            )
        total = total.astype(BF16)
        start = 0
        for out in outs:
            out[:, at] = total[start : start + out.shape[0]]
            start += out.shape[0]


def run_experts(near, far, w_in, w_out):
    parts = [*near, *far]
    size, packed = parts[0].shape
    total = size * len(parts)
    count, block, width = w_out.shape
    room = 2 * MIB + total * (2 * packed + 2 * count * block + 8 * chunks_of(width)[0])
    outs = [pltpu.VMEM((size, width), BF16) for _ in parts]
    results = pl.pallas_call(
        functools.partial(experts_kernel, len(parts), tuple(len(x) for x in w_in)),
        out_shape=outs,
        in_specs=[VMEM] * (len(parts) + sum(len(x) for x in w_in) + 1),
        out_specs=[VMEM] * len(outs),
        scratch_shapes=[
            pltpu.VMEM((total, packed), BF16),
            pltpu.VMEM((total, count * block), BF16),
        ],
        compiler_params=pltpu.CompilerParams(vmem_limit_bytes=room),
        cost_estimate=pl.CostEstimate(
            flops=6 * total * count * width * block, bytes_accessed=6 * count * width * block, transcendentals=0
        ),
        name="experts",
    )(*[in_vmem(x) for x in parts], *[in_vmem(w) for x in w_in for w in x], w_out)
    return results[: len(near)], results[len(near) :]


def add(*terms):
    total = terms[0].astype(F32)
    for term in terms[1:]:
        total = total + term.astype(F32)
    return total.astype(BF16)


def shards(
    tokens,
    routes,
    gate_weights,
    experts_in,
    experts_out,
    query_latent,
    query_rope,
    cache_latent,
    cache_rope,
    lengths,
):
    side, dev = lax.axis_size("side"), lax.axis_size("dev")
    chips = dev // 2
    count = tokens.shape[0]
    packed = pack(tokens, routes, gate_weights, experts_in.shape[0] * side)
    chunks = chunks_of(tokens.shape[1])[1]
    last = 1 if chunks > 2 else 0
    order = [*range(2, side), 1]
    along = [swap(packed, k, 0) for k in order]
    first = fetch(experts_in, 0, 0, chunks - last)
    *along, first = lax.optimization_barrier((*along, first))
    along = [packed] + [along[order.index(k)] for k in range(1, side)]
    along = jnp.concatenate(along)
    near = [along] + [swap(along, 0, 2 * k) for k in range(1, chips)]
    others = [fetch(experts_in, e, 0, chunks, experts_out) for e in range(1, experts_in.shape[0])]
    far = [swap(near[0], 0, 1)]
    near, others = lax.optimization_barrier((near, others))
    far += [swap(piece, 0, 1) for piece in near[1:]]
    weights = [[first]] + [[x] for x in others]
    if last:
        near, rest = lax.optimization_barrier((near, experts_in))
        weights[0].append(fetch(rest, 0, chunks - last, last))
    near_part, far_part = run_experts(near, far, weights, experts_out)
    both = [add(near_part[k], swap(far_part[k], 0, 1)) for k in range(1, chips)]
    own_far, both = lax.optimization_barrier((far_part[0], both))
    across = [swap(both[k - 1], 0, 2 * k) for k in range(1, chips)]
    own = add(near_part[0], swap(own_far, 0, 1))
    attended = attend(query_latent, query_rope, cache_latent, cache_rope, lengths)
    across, attended = lax.optimization_barrier((across, attended))
    column = add(own, *across)
    routed_out = add(
        column[:count],
        *[swap(column[k * count : (k + 1) * count], k, 0) for k in range(1, side)],
    )
    return (routed_out, attended)


def solution(mesh):
    return jax.shard_map(
        shards,
        mesh=mesh,
        in_specs=(
            P(("groups", "side", "dev"), None),
            P(("groups", "side", "dev"), None),
            P(("groups", "side", "dev"), None),
            P("side", None, None, "dev"),
            P("side", "dev", None),
            P(("groups", "side", "dev"), None, None),
            P(("groups", "side", "dev"), None, None),
            P(("groups", "side", "dev"), None, None),
            P(("groups", "side", "dev"), None, None),
            P(("groups", "side", "dev")),
        ),
        out_specs=(P(("groups", "side", "dev"), None), P(("groups", "side", "dev"), None, None)),
        check_vma=False,
    )
```

```python
import functools

import jax
import jax.numpy as jnp
from jax import lax
from jax.experimental import pallas as pl
from jax.experimental.pallas import tpu as pltpu
from jax.sharding import PartitionSpec as P

SCORE_SCALE = 192.0 ** (-0.5)
BF16 = jnp.bfloat16
F32 = jnp.float32
LANES = 128


def swap(x, side_bits, dev_bits):
    side, dev = lax.axis_size("side"), lax.axis_size("dev")
    if side_bits == 0:
        return lax.ppermute(x, "dev", [(i, i ^ dev_bits) for i in range(dev)])
    if dev_bits == 0:
        return lax.ppermute(x, "side", [(i, i ^ side_bits) for i in range(side)])
    pairs = [(i, i ^ (side_bits * dev + dev_bits)) for i in range(side * dev)]
    return lax.ppermute(x, ("side", "dev"), pairs)


def in_hbm(x):
    return pltpu.with_memory_space_constraint(x, pltpu.HBM)


def in_vmem(x):
    return pltpu.with_memory_space_constraint(x, pltpu.VMEM)


HBM = pl.BlockSpec(memory_space=pltpu.HBM)
VMEM = pl.BlockSpec(memory_space=pltpu.VMEM)
MIB = 1024 * 1024


def pack_kernel(tokens, routes, gates, out, routes_here, gates_here, sems):
    width = tokens.shape[1]
    pairs = ((tokens, out.at[:, :width]), (routes, routes_here), (gates, gates_here))
    copies = [pltpu.make_async_copy(a, b, sems.at[i]) for i, (a, b) in enumerate(pairs)]
    for copy in copies:
        copy.start()
    for copy in copies[1:]:
        copy.wait()
    lane = lax.broadcasted_iota(jnp.int32, (tokens.shape[0], out.shape[1] - width), 1)
    total = jnp.zeros(lane.shape, F32)
    gate = gates_here[...].astype(F32)
    for k in range(routes.shape[1]):
        total = total + jnp.where(routes_here[:, k : k + 1] == lane, gate[:, k : k + 1], 0.0)
    out[:, width:] = total.astype(BF16)
    copies[0].wait()


def pack(tokens, routes, gates, experts):
    rows, width = tokens.shape
    pad = -(-experts // LANES) * LANES
    arrays = (tokens, routes, gates)
    return pl.pallas_call(
        pack_kernel,
        out_shape=pltpu.VMEM((rows, width + pad), BF16),
        in_specs=[HBM] * 3,
        out_specs=VMEM,
        scratch_shapes=[pltpu.VMEM(x.shape, x.dtype) for x in arrays[1:]] + [pltpu.SemaphoreType.DMA((3,))],
        compiler_params=pltpu.CompilerParams(vmem_limit_bytes=2 * MIB),
        name="pack",
    )(*[in_hbm(x) for x in arrays])


def chunks_of(width):
    step = 1024 if width % 1024 == 0 else width
    return step, width // step


def fetch_kernel(e, first, w_in, *refs):
    held, sems = refs[-2:]
    step, _ = chunks_of(w_in.shape[2])
    copies = [
        pltpu.make_async_copy(
            w_in.at[e, g, pl.ds((first + i) * step, step)], held.at[g, pl.ds(i * step, step)], sems.at[g, i]
        )
        for i in range(held.shape[1] // step)
        for g in range(2)
    ]
    for copy in copies:
        copy.start()
    for copy in copies:
        copy.wait()


def fetch(w_in, e, first, count, *ready):
    _, _, width, block = w_in.shape
    step, _ = chunks_of(width)
    return pl.pallas_call(
        functools.partial(fetch_kernel, e, first),
        out_shape=pltpu.VMEM((2, count * step, block), BF16),
        in_specs=[HBM] + [VMEM] * len(ready),
        out_specs=VMEM,
        scratch_shapes=[pltpu.SemaphoreType.DMA((2, count))],
        compiler_params=pltpu.CompilerParams(vmem_limit_bytes=2 * MIB),
        name="fetch",
    )(in_hbm(w_in), *ready)


def attend_kernel(lengths, queries, rope_queries, latents, ropes, attended, q, qr, c, cr, out, sems, out_sems):
    pairs = ((queries, q), (rope_queries, qr), (latents, c), (ropes, cr))
    count = q.shape[0]
    copies = [
        [pltpu.make_async_copy(a.at[r], b.at[r], sems.at[r, i]) for i, (a, b) in enumerate(pairs)]
        for r in range(count)
    ]
    for request in copies:
        for copy in request:
            copy.start()
    results = []
    for r in range(count):
        for copy in copies[r]:
            copy.wait()
        latent = c[r]
        scores = lax.dot_general(
            q[r], latent, (((1,), (1,)), ((), ())), preferred_element_type=F32
        ) + lax.dot_general(qr[r], cr[r], (((0,), (0,)), ((), ())), preferred_element_type=F32)
        scores = scores * SCORE_SCALE
        place = lax.broadcasted_iota(jnp.int32, scores.shape, 1)
        scores = jnp.where(place < lengths[r], scores, -jnp.inf)
        shifted = jnp.exp(scores - jnp.max(scores, axis=1, keepdims=True))
        shares = (shifted / jnp.sum(shifted, axis=1, keepdims=True)).astype(BF16)
        out[r] = jnp.dot(shares, latent, preferred_element_type=F32).astype(BF16)
        results.append(pltpu.make_async_copy(out.at[r], attended.at[r], out_sems.at[r]))
        results[-1].start()
    for copy in results:
        copy.wait()


def attend(query_latent, query_rope, cache_latent, cache_rope, lengths):
    arrays = (query_latent, query_rope, cache_latent, cache_rope)
    count = query_latent.shape[0]
    return pl.pallas_call(
        attend_kernel,
        out_shape=pltpu.HBM(query_latent.shape, BF16),
        in_specs=[pl.BlockSpec(memory_space=pltpu.SMEM)] + [HBM] * 4,
        out_specs=HBM,
        scratch_shapes=[pltpu.VMEM(x.shape, BF16) for x in (*arrays, query_latent)]
        + [pltpu.SemaphoreType.DMA((count, 4)), pltpu.SemaphoreType.DMA((count,))],
        compiler_params=pltpu.CompilerParams(vmem_limit_bytes=8 * MIB),
        name="attend",
    )(in_hbm(lengths), *[in_hbm(x) for x in arrays])


def project(rows, parts, g):
    total, start = None, 0
    for part in parts:
        size = part.shape[1]
        term = jnp.dot(rows[:, start : start + size], part[g], preferred_element_type=F32)
        total = term if total is None else total + term
        start += size
    return total


def experts_kernel(pieces, held_parts, *refs):
    parts, refs = refs[:pieces], refs[pieces:]
    count = sum(held_parts)
    flat, held, outs = refs[:count], refs[count], refs[count + 1 : -2]
    rows, act = refs[-2:]
    w_in, start = [], 0
    for number in held_parts:
        w_in.append(flat[start : start + number])
        start += number
    count, block, width = held.shape
    step, chunks = chunks_of(width)
    size = parts[0].shape[0]
    for i, part in enumerate(parts):
        rows[i * size : (i + 1) * size, :] = part[...]
    first = lax.axis_index("side") * count
    gates = rows[:, width:].astype(F32)
    lane = lax.broadcasted_iota(jnp.int32, gates.shape, 1)
    for e in range(count):
        gate, up = [project(rows, w_in[e], g) for g in range(2)]
        weight = jnp.sum(jnp.where(lane == first + e, gates, 0.0), axis=1, keepdims=True)
        value = gate / (1.0 + jnp.exp(-gate)) * up * weight
        act[:, e * block : (e + 1) * block] = value.astype(BF16)
    for i in range(chunks):
        at = slice(i * step, (i + 1) * step)
        total = jnp.dot(act[:, :block], held[0, :, at], preferred_element_type=F32)
        for e in range(1, count):
            total = total + jnp.dot(
                act[:, e * block : (e + 1) * block], held[e, :, at], preferred_element_type=F32
            )
        total = total.astype(BF16)
        start = 0
        for out in outs:
            out[:, at] = total[start : start + out.shape[0]]
            start += out.shape[0]


def run_experts(near, far, w_in, w_out):
    parts = [*near, *far]
    size, packed = parts[0].shape
    total = size * len(parts)
    count, block, width = w_out.shape
    room = 2 * MIB + total * (2 * packed + 2 * count * block + 8 * chunks_of(width)[0])
    outs = [pltpu.VMEM((size, width), BF16) for _ in parts]
    results = pl.pallas_call(
        functools.partial(experts_kernel, len(parts), tuple(len(x) for x in w_in)),
        out_shape=outs,
        in_specs=[VMEM] * (len(parts) + sum(len(x) for x in w_in) + 1),
        out_specs=[VMEM] * len(outs),
        scratch_shapes=[
            pltpu.VMEM((total, packed), BF16),
            pltpu.VMEM((total, count * block), BF16),
        ],
        compiler_params=pltpu.CompilerParams(vmem_limit_bytes=room),
        cost_estimate=pl.CostEstimate(
            flops=6 * total * count * width * block, bytes_accessed=6 * count * width * block, transcendentals=0
        ),
        name="experts",
    )(*[in_vmem(x) for x in parts], *[in_vmem(w) for x in w_in for w in x], w_out)
    return results[: len(near)], results[len(near) :]


def add(*terms):
    total = terms[0].astype(F32)
    for term in terms[1:]:
        total = total + term.astype(F32)
    return total.astype(BF16)


def shards(
    tokens,
    routes,
    gate_weights,
    experts_in,
    experts_out,
    query_latent,
    query_rope,
    cache_latent,
    cache_rope,
    lengths,
):
    side, dev = lax.axis_size("side"), lax.axis_size("dev")
    chips = dev // 2
    count = tokens.shape[0]
    packed = pack(tokens, routes, gate_weights, experts_in.shape[0] * side)
    chunks = chunks_of(tokens.shape[1])[1]
    last = 2 if chunks > 2 else 0
    order = [*range(2, side), 1]
    along = [swap(packed, k, 0) for k in order]
    first = fetch(experts_in, 0, 0, chunks - last)
    *along, first = lax.optimization_barrier((*along, first))
    along = [packed] + [along[order.index(k)] for k in range(1, side)]
    along = jnp.concatenate(along)
    near = [along] + [swap(along, 0, 2 * k) for k in range(1, chips)]
    others = [fetch(experts_in, e, 0, chunks, experts_out) for e in range(1, experts_in.shape[0])]
    far = [swap(near[0], 0, 1)]
    near, others = lax.optimization_barrier((near, others))
    far += [swap(piece, 0, 1) for piece in near[1:]]
    weights = [[first]] + [[x] for x in others]
    if last:
        near, rest = lax.optimization_barrier((near, experts_in))
        weights[0].append(fetch(rest, 0, chunks - last, last))
    near_part, far_part = run_experts(near, far, weights, experts_out)
    both = [add(near_part[k], swap(far_part[k], 0, 1)) for k in range(1, chips)]
    own_far, both = lax.optimization_barrier((far_part[0], both))
    across = [swap(both[k - 1], 0, 2 * k) for k in range(1, chips)]
    own = add(near_part[0], swap(own_far, 0, 1))
    attended = attend(query_latent, query_rope, cache_latent, cache_rope, lengths)
    across, attended = lax.optimization_barrier((across, attended))
    column = add(own, *across)
    routed_out = add(
        column[:count],
        *[swap(column[k * count : (k + 1) * count], k, 0) for k in range(1, side)],
    )
    return (routed_out, attended)


def solution(mesh):
    return jax.shard_map(
        shards,
        mesh=mesh,
        in_specs=(
            P(("groups", "side", "dev"), None),
            P(("groups", "side", "dev"), None),
            P(("groups", "side", "dev"), None),
            P("side", None, None, "dev"),
            P("side", "dev", None),
            P(("groups", "side", "dev"), None, None),
            P(("groups", "side", "dev"), None, None),
            P(("groups", "side", "dev"), None, None),
            P(("groups", "side", "dev"), None, None),
            P(("groups", "side", "dev")),
        ),
        out_specs=(P(("groups", "side", "dev"), None), P(("groups", "side", "dev"), None, None)),
        check_vma=False,
    )
```
